32 devices in a mesh: tm: 4 (over y, core), space: 8 (over z, x).
Axes of the slice: x: 2, y: 2, z: 4, core: 2. Of those that a mesh axis runs over, the one named last changes fastest.
Arguments:
- features: bfloat16 [8, 64, 128, 256], P('tm', 'space'), may hold values from -6 to 6
- clip_frames: int32 [2], replicated, may hold values from 1 to 4, as said below
- band_maps: int32 [3, 8], replicated, may hold values from 0 to 7, each once within a row
- gain_one: float32 [256], replicated, may hold values from 0.1 to 1.9
- conv_one: bfloat16 [3, 3, 3, 256, 256], replicated, may hold values from -0.078125 to 0.078125
- gain_two: float32 [256], replicated, may hold values from 0.1 to 1.9
- conv_two: bfloat16 [3, 3, 3, 256, 256], replicated, may hold values from -0.078125 to 0.078125
- gain_out: float32 [256], replicated, may hold values from 0.1 to 1.9
- latent_weight: bfloat16 [256, 16], replicated, may hold values from -0.375 to 0.375
- embed_weight: bfloat16 [64, 3072], replicated, may hold values from -0.75 to 0.75
Outputs:
- tokens_fine: bfloat16 [8, 8, 32, 8, 3072], P('tm', 'space')
- tokens_mid: bfloat16 [8, 8, 16, 4, 3072], P('tm', 'space')
- tokens_coarse: bfloat16 [8, 8, 8, 2, 3072], P('tm', 'space')
The draws below stay inside these ranges and needn't reach their ends.
Inputs may be any that keep to these rules, and one draw needn't show every extreme that they name: `clip_frames`: one clip has exactly 4 real frames and the other fewer. `band_maps`: each row is a permutation of the 8 bands.
All inputs are finite; a program needn't handle non-finite values.
Results may differ from the reference program's by a relative error of at most 0.011.
Values may be sent and summed in bfloat16 or wider, within the bound.
A program may use at most 128 MiB of HBM per device.

```python
import jax
import jax.numpy as jnp
from jax import lax

C = 256
LC = 16
HID = 3072
COLS = 128
FRAMES = 8
FMAX = 4
ROWS = 64
BANDS = 8


def draw_clip_frames(key, part):
    key = jax.random.fold_in(key, 7)
    first_key = jax.random.fold_in(key, 1)
    second_key = jax.random.fold_in(key, 2)
    longer = jax.random.randint(first_key, (), 0, 2, dtype=jnp.int32)
    shorter = jax.random.randint(second_key, (), 1, FMAX, dtype=jnp.int32)
    slots = jnp.arange(2, dtype=jnp.int32)
    return jnp.where(slots == longer, FMAX, shorter).astype(jnp.int32)


def level_of(own_key, shape, pieces, low, largest):
    def one(dim, blocks):
        draws = jax.random.uniform(jax.random.fold_in(jax.random.fold_in(own_key, 6), dim), (blocks,), jnp.float32, low / len(pieces), largest / len(pieces))
        return jnp.repeat(jnp.exp(draws), shape[dim] // blocks).reshape((-1,) + (1,) * (len(shape) - dim - 1))

    factor_of = one(*pieces[0])
    for cut in pieces[1:]:
        factor_of = factor_of * one(*cut)
    return factor_of


def scatter_about(stream_key, shape, spread, bound, split=(), kind=jnp.bfloat16):
    values = jax.random.normal(stream_key, shape, jnp.float32) * spread
    if len(split) > 0:
        values = level_of(stream_key, shape, split, -0.22, 0.18) * values
    return jnp.clip(values, min=-bound, max=bound).astype(kind)


def setup_inputs(seed: int = 0) -> dict:
    key_of = jax.random.split(jax.random.key(seed), 11)
    return {
        "features": scatter_about(key_of[0], (FRAMES, ROWS, COLS, C), 1.0, 6.0, ((0, 4), (1, 8))),
        "clip_frames": draw_clip_frames(jax.random.fold_in(key_of[10], 71), 0),
        "band_maps": jax.vmap(lambda own: jax.random.permutation(own, BANDS))(jax.random.split(key_of[2], 3)).reshape((3, BANDS)).astype(jnp.int32),
        "gain_one": jnp.clip(1.0 + 0.18 * jax.random.normal(key_of[3], (C,), jnp.float32), 0.1, 1.9),
        "conv_one": scatter_about(key_of[4], (3, 3, 3, C, C), (27 * C) ** -0.5, 0.078125),
        "gain_two": jnp.clip(1.0 + 0.18 * jax.random.normal(key_of[5], (C,), jnp.float32), 0.1, 1.9),
        "conv_two": scatter_about(key_of[6], (3, 3, 3, C, C), (27 * C) ** -0.5, 0.078125),
        "gain_out": jnp.clip(1.0 + 0.18 * jax.random.normal(key_of[7], (C,), jnp.float32), 0.1, 1.9),
        "latent_weight": scatter_about(key_of[8], (C, LC), C ** -0.5, 0.375),
        "embed_weight": scatter_about(key_of[9], (4 * LC, HID), (4 * LC) ** -0.5, 0.75),
    }


def activate(stream, gain_vec):
    values = stream.astype(jnp.float32)
    meansq = lax.optimization_barrier(jnp.mean(values * values, axis=-1, keepdims=True))
    return jax.nn.silu(values * lax.rsqrt(meansq + 1e-06) * gain_vec)

def clip_conv(activated, weight):
    channels = activated.shape[-1]
    clips = activated.reshape(2, FMAX, ROWS, COLS, channels)
    padded = jnp.pad(clips, ((0, 0), (2, 0), (1, 1), (1, 1), (0, 0)))
    running = jnp.zeros((2 * FMAX * ROWS * COLS, weight.shape[-1]), jnp.float32)
    for tap_time in range(3):
        for tap_row in range(3):
            window_rows = padded[:, tap_time:tap_time + FMAX, tap_row:tap_row + ROWS]
            stacked = jnp.concatenate([window_rows[:, :, :, 0:COLS], window_rows[:, :, :, 1:COLS + 1], window_rows[:, :, :, 2:COLS + 2]], axis=-1)
            kernel = weight[tap_time, tap_row].reshape(3 * channels, -1)
            running = running + jnp.dot(stacked.reshape(-1, 3 * channels), kernel, preferred_element_type=jnp.float32)
    return running.reshape(FRAMES, ROWS, COLS, -1)

def level_tokens(latent, factor, band_order, valid, embed_weight):
    frames, rows, cols, lat = latent.shape
    pooled = latent.reshape(frames, rows // factor, factor, cols // factor, factor, lat).mean(axis=(2, 4))
    patch_rows = rows // factor // 2
    patch_cols = cols // factor // 2
    patches = pooled.reshape(frames, patch_rows, 2, patch_cols, 2, lat).transpose(0, 1, 3, 2, 4, 5)
    patches = patches.reshape(frames, patch_rows, patch_cols, 4 * lat).astype(jnp.bfloat16)
    patches = jnp.where(valid[:, None, None, None], patches, jnp.zeros_like(patches))
    embedded = jnp.dot(patches.reshape(-1, 4 * lat), embed_weight, preferred_element_type=jnp.float32)
    embedded = embedded.astype(jnp.bfloat16).reshape(frames, patch_rows, BANDS, patch_cols // BANDS, -1)
    embedded = jnp.take(embedded, band_order, axis=2)
    return embedded.transpose(0, 2, 1, 3, 4)

def reference(features, clip_frames, band_maps, gain_one, conv_one, gain_two, conv_two, gain_out, latent_weight, embed_weight):
    stream = features
    for gain_vec, weight in ((gain_one, conv_one), (gain_two, conv_two)):
        activated = activate(stream, gain_vec).astype(jnp.bfloat16)
        stream = (stream.astype(jnp.float32) + clip_conv(activated, weight)).astype(jnp.bfloat16)
    final_act = activate(stream, gain_out).astype(jnp.bfloat16)
    latent = jnp.dot(final_act.reshape(-1, C), latent_weight, preferred_element_type=jnp.float32).reshape(FRAMES, ROWS, COLS, LC)
    slot_ids = jnp.arange(FRAMES, dtype=jnp.int32)
    clip_ids = slot_ids // FMAX
    limits = jnp.where(clip_ids == 0, clip_frames[0], clip_frames[1])
    valid = slot_ids - clip_ids * FMAX < limits
    tokens_fine = level_tokens(latent, 1, band_maps[0], valid, embed_weight)
    tokens_mid = level_tokens(latent, 2, band_maps[1], valid, embed_weight)
    tokens_coarse = level_tokens(latent, 4, band_maps[2], valid, embed_weight)
    return (tokens_fine, tokens_mid, tokens_coarse)
```

```python
import jax
import jax.numpy as jnp
from jax import lax
from jax.sharding import PartitionSpec as P


def from_behind(array, axis, by):
    peers = lax.axis_size(axis)
    pairs = [(i, i + by) for i in range(peers) if 0 <= i + by < peers]
    return lax.ppermute(array, axis, pairs)


def with_halo(cells, sides, width):
    for axis, dim in sides:
        count = lax.axis_size(axis)
        ends = count - 1
        head = lax.slice_in_dim(cells, 0, width, axis=dim)
        tail = lax.slice_in_dim(cells, cells.shape[dim] - width, cells.shape[dim], axis=dim)
        cells = jnp.concatenate(
            [
                lax.ppermute(tail, axis, [(i, (i + 1) % count) for i in range(ends)]),
                cells,
                lax.ppermute(head, axis, [((i + 1) % count, i) for i in range(ends)]),
            ],
            axis=dim,
        )
    return cells


def activate(stream, gain_vec):
    values = stream.astype(jnp.float32)
    meansq = jnp.mean(values * values, axis=-1, keepdims=True)
    return jax.nn.silu(values * lax.rsqrt(meansq + 1e-06) * gain_vec)


def causal_conv(bordered, weight, frame_ids, clip_len):
    out_frames = bordered.shape[0] - 2
    out_rows = bordered.shape[1] - 2
    col_count = bordered.shape[2]
    channels = bordered.shape[3]
    widened = jnp.pad(bordered, ((0, 0), (0, 0), (1, 1), (0, 0)))
    position = jnp.mod(frame_ids, clip_len)
    running = jnp.zeros((out_frames, out_rows, col_count, weight.shape[-1]), jnp.float32)
    for tap_time in range(3):
        keep_mask = (position >= 2 - tap_time)[:, None, None, None]
        for tap_row in range(3):
            window_rows = widened[tap_time : tap_time + out_frames, tap_row : tap_row + out_rows]
            stacked = jnp.concatenate(
                [
                    window_rows[:, :, 0:col_count],
                    window_rows[:, :, 1 : col_count + 1],
                    window_rows[:, :, 2 : col_count + 2],
                ],
                axis=-1,
            )
            stacked = jnp.where(keep_mask, stacked, jnp.zeros_like(stacked))
            kernel = weight[tap_time, tap_row].reshape(3 * channels, -1)
            running = running + jnp.einsum(
                "frwk,ko->frwo", stacked, kernel, preferred_element_type=jnp.float32
            )
    return running


def section_each(stream, gain_vec, weight, frame_ids, clip_len):
    activated = activate(stream, gain_vec).astype(jnp.bfloat16)
    earlier = from_behind(activated, "tm", 1)
    extended = jnp.concatenate([earlier, activated], axis=0)
    bordered = with_halo(extended, (("space", 1),), 1)
    update = causal_conv(bordered, weight, frame_ids, clip_len)
    return (stream.astype(jnp.float32) + update).astype(jnp.bfloat16)


def level_patches(latent, factor, band_order, valid, bands):
    frames, rows, cols, lat = latent.shape
    pooled = latent.reshape(frames, rows // factor, factor, cols // factor, factor, lat).mean(
        axis=(2, 4)
    )
    patch_rows = rows // factor // 2
    patch_cols = cols // factor // 2
    patches = pooled.reshape(frames, patch_rows, 2, patch_cols, 2, lat).transpose(0, 1, 3, 2, 4, 5)
    patches = patches.reshape(frames, patch_rows, patch_cols, 4 * lat).astype(jnp.bfloat16)
    patches = jnp.where(valid[:, None, None, None], patches, jnp.zeros_like(patches))
    grouped = patches.reshape(frames, patch_rows, bands, patch_cols // bands, 4 * lat)
    return jnp.take(grouped, band_order, axis=2).transpose(0, 2, 1, 3, 4)


def embed_tokens(grouped, embed_weight):
    embedded = jnp.einsum(
        "fbrcp,ph->fbrch", grouped, embed_weight, preferred_element_type=jnp.float32
    )
    return embedded.astype(jnp.bfloat16)


def settle(moved):
    frames, bands, rows, cols, hidden = moved.shape
    return moved.reshape(frames, 1, bands * rows, cols, hidden)


def body(
    features,
    clip_frames,
    band_maps,
    gain_one,
    conv_one,
    gain_two,
    conv_two,
    gain_out,
    latent_weight,
    embed_weight,
):
    frames_here = features.shape[0]
    clip_len = frames_here * lax.axis_size("tm") // 2
    bands = lax.axis_size("space")
    first_slot = lax.axis_index("tm") * frames_here
    frame_ids = first_slot + jnp.arange(frames_here, dtype=jnp.int32)
    stream = section_each(features, gain_one, conv_one, frame_ids, clip_len)
    stream = section_each(stream, gain_two, conv_two, frame_ids, clip_len)
    final_act = activate(stream, gain_out).astype(jnp.bfloat16)
    latent = jnp.einsum(
        "frwc,cl->frwl", final_act, latent_weight, preferred_element_type=jnp.float32
    )
    clip_ids = frame_ids // clip_len
    limits = jnp.where(clip_ids == 0, clip_frames[0], clip_frames[1])
    valid = frame_ids - clip_ids * clip_len < limits
    patch_zero = level_patches(latent, 1, band_maps[0], valid, bands)
    patch_one = level_patches(latent, 2, band_maps[1], valid, bands)
    patch_two = level_patches(latent, 4, band_maps[2], valid, bands)
    parts = (patch_zero, patch_one, patch_two)
    flat = jnp.concatenate(
        [p.transpose(1, 0, 2, 3, 4).reshape(bands, -1) for p in parts], axis=1
    )
    moved = lax.all_to_all(flat, "space", split_axis=0, concat_axis=0, tiled=True)
    results = []
    start = 0
    for p in parts:
        frames, _, rows, cols, depth = p.shape
        size = frames * rows * cols * depth
        piece = moved[:, start : start + size].reshape(bands, frames, rows, cols, depth)
        start += size
        results.append(embed_tokens(piece.transpose(1, 0, 2, 3, 4), embed_weight))
    return (settle(results[0]), settle(results[1]), settle(results[2]))


def solution(mesh):
    return jax.shard_map(
        body,
        mesh=mesh,
        in_specs=(P("tm", "space", None, None), P(), P(), P(), P(), P(), P(), P(), P(), P()),
        out_specs=(
            P("tm", "space", None, None, None),
            P("tm", "space", None, None, None),
            P("tm", "space", None, None, None),
        ),
        check_vma=False,
    )
```

```python
import functools

import jax
import jax.numpy as jnp
from jax import lax
from jax.experimental import pallas as pl
from jax.experimental.pallas import tpu as pltpu
from jax.sharding import PartitionSpec as P

MESH = pl.DeviceIdType.MESH
ROW_BLOCK = 2


def activate(values, gain_row):
    meansq = jnp.mean(values * values, axis=-1, keepdims=True)
    half = values * lax.rsqrt(meansq + 1e-06) * (gain_row * 0.5)
    return half + half * jnp.tanh(half)


def encoder_kernel(
    clip_len,
    bands,
    clip_ref,
    maps_ref,
    x_ref,
    gains_ref,
    lat_ref,
    w1_hbm,
    w2_hbm,
    out_ref,
    w_one,
    w_two,
    ext_one,
    ext_two,
    mid_stream,
    lat_rows,
    fine_rows,
    mid_rows,
    coarse_rows,
    pool_mid,
    pool_coarse,
    fine_bands,
    mid_bands,
    coarse_bands,
    stage,
    send_buf,
    recv_buf,
    w_sem,
    halo_send,
    halo_recv,
    band_send,
    band_recv,
):
    frames, rows, cols, chans = x_ref.shape
    time = lax.axis_index("tm")
    place = lax.axis_index("space")
    first = time * frames
    has_prev = lax.rem(first, clip_len) != 0
    has_next = lax.rem(first + frames, clip_len) != 0
    has_up = place > 0
    has_down = place < bands - 1

    weight_copies = [
        [
            pltpu.make_async_copy(src.at[:, kx], dst.at[kx], w_sem.at[sec, kx])
            for kx in range(3)
        ]
        for sec, (src, dst) in enumerate(((w1_hbm, w_one), (w2_hbm, w_two)))
    ]
    for group in weight_copies:
        for copy in group:
            copy.start()

    barrier = pltpu.get_barrier_semaphore()
    links = [
        (has_next, time + 1, place),
        (has_prev, time - 1, place),
        (has_next & has_up, time + 1, place - 1),
        (has_next & has_down, time + 1, place + 1),
        (has_prev & has_up, time - 1, place - 1),
        (has_prev & has_down, time - 1, place + 1),
    ]
    for there, t, s in links:

        @pl.when(there)
        def _():
            pl.semaphore_signal(
                barrier, inc=1, device_id={"tm": t, "space": s}, device_id_type=MESH
            )

    for step in range(1, bands):
        pl.semaphore_signal(
            barrier,
            inc=1,
            device_id={"tm": time, "space": lax.rem(place + step, bands)},
            device_id_type=MESH,
        )

    gain_one = gains_ref[0:1, :]
    gain_two = gains_ref[1:2, :]
    gain_out = gains_ref[2:3, :]

    for ext in (ext_one, ext_two):

        @pl.when(jnp.logical_not(has_prev))
        def _():
            ext[0:2] = jnp.zeros((2, rows + 2, cols, chans), jnp.bfloat16)

        @pl.when(jnp.logical_not(has_up))
        def _():
            ext[:, 0] = jnp.zeros((frames + 2, cols, chans), jnp.bfloat16)

        @pl.when(jnp.logical_not(has_down))
        def _():
            ext[:, rows + 1] = jnp.zeros((frames + 2, cols, chans), jnp.bfloat16)

    @pl.loop(0, rows)
    def _(r):
        for f in range(frames):
            values = x_ref[f, r].astype(jnp.float32)
            ext_one[2 + f, r + 1] = activate(values, gain_one).astype(jnp.bfloat16)

    peers = bands - 1
    for there, _, _ in links:
        peers = peers + jnp.where(there, 1, 0)
    pl.semaphore_wait(barrier, peers)

    def halo(sec, ext):
        sends = (
            (has_next, ext.at[frames : frames + 2, 1 : rows + 1], ext.at[0:2, 1 : rows + 1], 1, 0),
            (has_up, ext.at[2 : frames + 2, 1], ext.at[2 : frames + 2, rows + 1], 0, -1),
            (has_down, ext.at[2 : frames + 2, rows], ext.at[2 : frames + 2, 0], 0, 1),
            (has_next & has_up, ext.at[frames : frames + 2, 1], ext.at[0:2, rows + 1], 1, -1),
            (has_next & has_down, ext.at[frames : frames + 2, rows], ext.at[0:2, 0], 1, 1),
        )
        waits = (has_prev, has_down, has_up, has_prev & has_down, has_prev & has_up)
        made = []
        for k, (there, src, dst, dt, ds) in enumerate(sends):
            copy = pltpu.make_async_remote_copy(
                src_ref=src,
                dst_ref=dst,
                send_sem=halo_send.at[sec, k],
                recv_sem=halo_recv.at[sec, k],
                device_id={"tm": time + dt, "space": place + ds},
                device_id_type=MESH,
            )
            made.append((there, waits[k], copy))
        return made

    def start_all(made):
        for k in (1, 2, 3, 4, 0):
            there, _, copy = made[k]

            @pl.when(there)
            def _():
                copy.start()

    def finish_recv(made):
        for _, here, copy in made:

            @pl.when(here)
            def _():
                copy.wait_recv()

    def finish_send(made):
        for there, _, copy in made:

            @pl.when(there)
            def _():
                copy.wait_send()

    col_id = lax.broadcasted_iota(jnp.int32, (cols, chans), 0)
    size = ROW_BLOCK * cols

    def conv_rows(ext, weight, r0, f):
        lhs = jnp.concatenate(
            [
                ext[f + kt, pl.ds(r0 + ky, ROW_BLOCK)].reshape(size, chans)
                for kt in range(3)
                for ky in range(3)
            ],
            axis=1,
        )
        taps = [
            jnp.dot(
                lhs,
                weight[kx].reshape(9 * chans, chans),
                preferred_element_type=jnp.float32,
            )
            for kx in range(3)
        ]
        done = []
        for k in range(ROW_BLOCK):
            left, mid, right = (tap[k * cols : (k + 1) * cols] for tap in taps)
            left = jnp.where(col_id == 0, 0.0, pltpu.roll(left, 1, 0))
            right = jnp.where(col_id == cols - 1, 0.0, pltpu.roll(right, cols - 1, 0))
            done.append(mid + left + right)
        return done

    halo_one = halo(0, ext_one)
    start_all(halo_one)
    for copy in weight_copies[0]:
        copy.wait()
    finish_recv(halo_one)

    @pl.loop(0, rows // ROW_BLOCK)
    def _(block):
        r0 = block * ROW_BLOCK
        for f in range(frames):
            for k, update in enumerate(conv_rows(ext_one, w_one, r0, f)):
                total = x_ref[f, r0 + k].astype(jnp.float32) + update
                rounded = total.astype(jnp.bfloat16)
                mid_stream[f, r0 + k] = rounded
                ext_two[2 + f, r0 + k + 1] = activate(
                    rounded.astype(jnp.float32), gain_two
                ).astype(jnp.bfloat16)

    halo_two = halo(1, ext_two)
    start_all(halo_two)
    for copy in weight_copies[1]:
        copy.wait()
    finish_recv(halo_two)

    @pl.loop(0, rows // ROW_BLOCK)
    def _(block):
        r0 = block * ROW_BLOCK
        latents = [jnp.zeros((cols, 128), jnp.float32)] * ROW_BLOCK
        for f in range(frames):
            for k, update in enumerate(conv_rows(ext_two, w_two, r0, f)):
                total = mid_stream[f, r0 + k].astype(jnp.float32) + update
                final = activate(
                    total.astype(jnp.bfloat16).astype(jnp.float32), gain_out
                ).astype(jnp.bfloat16)
                latents[k] = latents[k] + jnp.dot(
                    final, lat_ref[f], preferred_element_type=jnp.float32
                )
        for k in range(ROW_BLOCK):
            lat_rows[r0 + k] = latents[k]

    finish_send(halo_one)
    finish_send(halo_two)

    clip = lax.div(first, clip_len)
    limit = clip_ref[clip]

    def pyramid(source, count, width, patch_rows, pooled):
        lane = lax.broadcasted_iota(jnp.int32, (width, 128), 1)
        group = lax.rem(lax.div(lane, 16), 4)
        position = first - clip * clip_len + lax.div(lane, 64)
        keep = position < limit
        for i in range(count):
            total = None
            chosen = None
            for p in range(2):
                for q in range(2):
                    part = source[2 * i + p, pl.ds(q, width, stride=2), :]
                    total = part if total is None else total + part
                    chosen = (
                        part
                        if chosen is None
                        else jnp.where(group == 2 * p + q, part, chosen)
                    )
            patch_rows[i] = jnp.where(keep, chosen, 0.0)
            if pooled is not None:
                pooled[i] = total * 0.25

    levels = (
        (lat_rows, fine_rows, pool_mid, fine_bands),
        (pool_mid, mid_rows, pool_coarse, mid_bands),
        (pool_coarse, coarse_rows, None, coarse_bands),
    )
    stage[...] = jnp.zeros_like(stage)
    offset = 0
    for level, (source, patch_rows, pooled, by_band) in enumerate(levels):
        count, width, _ = patch_rows.shape
        pyramid(source, count, width, patch_rows, pooled)
        each = width // bands
        for b in range(bands):
            for i in range(count):
                by_band[b, i * each : (i + 1) * each] = patch_rows[
                    i, b * each : (b + 1) * each
                ]
        for d in range(bands):
            stage[d, offset : offset + count * each] = by_band[maps_ref[level, d]]
        offset += count * each
    for d in range(bands):
        send_buf[d] = stage[d].astype(jnp.bfloat16)

    moves = []
    for step in range(1, bands):
        target = lax.rem(place + step, bands)
        copy = pltpu.make_async_remote_copy(
            src_ref=send_buf.at[target],
            dst_ref=recv_buf.at[place],
            send_sem=band_send.at[step - 1],
            recv_sem=band_recv.at[step - 1],
            device_id={"tm": time, "space": target},
            device_id_type=MESH,
        )
        copy.start()
        moves.append(copy)
    recv_buf[place] = send_buf[place]
    for copy in moves:
        copy.wait_recv()
    for copy in moves:
        copy.wait_send()
    out_ref[...] = recv_buf[...]


def encode(features, clip_frames, band_maps, gains, latents, conv_one, conv_two, clip_len):
    bands = lax.axis_size("space")
    frames, rows, cols, chans = features.shape
    counts = [
        (rows // s // 2, cols // s // 2) for s in (1, 2, 4)
    ]
    used = sum(n * w // bands for n, w in counts)
    message = -(-used // 16) * 16
    f32, bf16 = jnp.float32, jnp.bfloat16
    vmem = pl.BlockSpec(memory_space=pltpu.VMEM)
    smem = pl.BlockSpec(memory_space=pltpu.SMEM)
    hbm = pl.BlockSpec(memory_space=pl.ANY)
    weight = pltpu.VMEM((3, 9, chans, chans), bf16)
    ext = pltpu.VMEM((frames + 2, rows + 2, cols, chans), bf16)
    scratch = [weight, weight, ext, ext, pltpu.VMEM((frames, rows, cols, chans), bf16)]
    scratch.append(pltpu.VMEM((rows, cols, 128), f32))
    scratch += [pltpu.VMEM((n, w, 128), f32) for n, w in counts]
    scratch += [pltpu.VMEM((n, w, 128), f32) for n, w in counts[:2]]
    scratch += [pltpu.VMEM((bands, n * w // bands, 128), f32) for n, w in counts]
    scratch += [
        pltpu.VMEM((bands, message, 128), f32),
        pltpu.VMEM((bands, message, 128), bf16),
        pltpu.VMEM((bands, message, 128), bf16),
        pltpu.SemaphoreType.DMA((2, 3)),
        pltpu.SemaphoreType.DMA((2, 5)),
        pltpu.SemaphoreType.DMA((2, 5)),
        pltpu.SemaphoreType.DMA((bands - 1,)),
        pltpu.SemaphoreType.DMA((bands - 1,)),
    ]
    return pl.pallas_call(
        functools.partial(encoder_kernel, clip_len, bands),
        out_shape=jax.ShapeDtypeStruct((bands, message, 128), bf16),
        in_specs=[smem, smem, vmem, vmem, vmem, hbm, hbm],
        out_specs=vmem,
        scratch_shapes=scratch,
        compiler_params=pltpu.CompilerParams(
            collective_id=0, has_side_effects=True, vmem_limit_bytes=52 * 1024 * 1024
        ),
        name="encoder",
    )(clip_frames, band_maps, features, gains, latents, conv_one, conv_two)


def body(
    features,
    clip_frames,
    band_maps,
    gain_one,
    conv_one,
    gain_two,
    conv_two,
    gain_out,
    latent_weight,
    embed_weight,
):
    frames, rows, cols, chans = features.shape
    clip_len = frames * lax.axis_size("tm") // 2
    bands = lax.axis_size("space")
    gains = jnp.stack([gain_one, gain_two, gain_out])
    repeated = jnp.tile(latent_weight, (1, 4))
    blank = jnp.zeros_like(repeated)
    latents = jnp.stack(
        [
            jnp.concatenate([repeated, blank], axis=1),
            jnp.concatenate([blank, repeated], axis=1),
        ]
    )
    moved = encode(
        features,
        clip_frames,
        band_maps,
        gains,
        latents,
        conv_one.reshape(9, 3, chans, chans),
        conv_two.reshape(9, 3, chans, chans),
        clip_len,
    )
    depth = embed_weight.shape[0]
    results = []
    start = 0
    for s in (1, 2, 4):
        count, each = rows // s // 2, cols // s // 2 // bands
        piece = moved[:, start : start + count * each]
        start += count * each
        piece = piece.reshape(bands * count, each, frames, depth).transpose(2, 0, 1, 3)
        embedded = jnp.einsum(
            "fice,eh->fich", piece, embed_weight, preferred_element_type=jnp.float32
        ).astype(jnp.bfloat16)
        results.append(embedded[:, None])
    return tuple(results)


def solution(mesh):
    return jax.shard_map(
        body,
        mesh=mesh,
        in_specs=(P("tm", "space", None, None), P(), P(), P(), P(), P(), P(), P(), P(), P()),
        out_specs=(
            P("tm", "space", None, None, None),
            P("tm", "space", None, None, None),
            P("tm", "space", None, None, None),
        ),
        check_vma=False,
    )
```

```python
import functools

import jax
import jax.numpy as jnp
from jax import lax
from jax.experimental import pallas as pl
from jax.experimental.pallas import tpu as pltpu
from jax.sharding import PartitionSpec as P

MESH = pl.DeviceIdType.MESH
ROW_BLOCK = 4


def activate(values, gain_row):
    meansq = jnp.mean(values * values, axis=-1, keepdims=True)
    half = values * lax.rsqrt(meansq + 1e-06) * (gain_row * 0.5)
    return half + half * jnp.tanh(half)


def encoder_kernel(
    clip_len,
    bands,
    clip_hbm,
    maps_hbm,
    x_hbm,
    g1_hbm,
    g2_hbm,
    g3_hbm,
    lat_hbm,
    w1_hbm,
    w2_hbm,
    fine_out,
    mid_out,
    coarse_out,
    clip_ref,
    maps_ref,
    x_ref,
    g1_ref,
    g2_ref,
    g3_ref,
    lat_in,
    lat_ref,
    w_one,
    w_two,
    ext_one,
    ext_two,
    mid_stream,
    lat_rows,
    fine_rows,
    mid_rows,
    coarse_rows,
    pool_mid,
    pool_coarse,
    fine_bands,
    mid_bands,
    coarse_bands,
    stage,
    send_buf,
    recv_buf,
    in_sem,
    w_sem,
    halo_send,
    halo_recv,
    band_send,
    band_recv,
):
    frames, rows, cols, chans = x_ref.shape
    time = lax.axis_index("tm")
    place = lax.axis_index("space")
    first = time * frames
    has_prev = lax.rem(first, clip_len) != 0
    has_next = lax.rem(first + frames, clip_len) != 0
    has_up = place > 0
    has_down = place < bands - 1

    weight_copies = [
        [
            pltpu.make_async_copy(src.at[:, kx], dst.at[kx], w_sem.at[sec, kx])
            for kx in range(3)
        ]
        for sec, (src, dst) in enumerate(((w1_hbm, w_one), (w2_hbm, w_two)))
    ]
    pairs = (
        (x_hbm, x_ref),
        (g1_hbm, g1_ref),
        (g2_hbm, g2_ref),
        (g3_hbm, g3_ref),
        (lat_hbm, lat_in),
        (clip_hbm, clip_ref),
        (maps_hbm, maps_ref),
    )
    small_copies = [
        pltpu.make_async_copy(src, dst, in_sem.at[k]) for k, (src, dst) in enumerate(pairs)
    ]
    for copy in small_copies:
        copy.start()
    for group in weight_copies:
        for copy in group:
            copy.start()

    barrier = pltpu.get_barrier_semaphore()
    links = [
        (has_next, time + 1, place),
        (has_prev, time - 1, place),
        (has_next & has_up, time + 1, place - 1),
        (has_next & has_down, time + 1, place + 1),
        (has_prev & has_up, time - 1, place - 1),
        (has_prev & has_down, time - 1, place + 1),
    ]
    for there, t, s in links:

        @pl.when(there)
        def _():
            pl.semaphore_signal(
                barrier, inc=1, device_id={"tm": t, "space": s}, device_id_type=MESH
            )

    for step in range(1, bands):
        pl.semaphore_signal(
            barrier,
            inc=1,
            device_id={"tm": time, "space": lax.rem(place + step, bands)},
            device_id_type=MESH,
        )

    for ext in (ext_one, ext_two):

        @pl.when(jnp.logical_not(has_prev))
        def _():
            ext[0:2] = jnp.zeros((2, rows + 2, cols, chans), jnp.bfloat16)

        @pl.when(jnp.logical_not(has_up))
        def _():
            ext[:, 0] = jnp.zeros((frames + 2, cols, chans), jnp.bfloat16)

        @pl.when(jnp.logical_not(has_down))
        def _():
            ext[:, rows + 1] = jnp.zeros((frames + 2, cols, chans), jnp.bfloat16)

    for copy in small_copies:
        copy.wait()
    gain_one = g1_ref[...]
    gain_two = g2_ref[...]
    gain_out = g3_ref[...]

    lat_count = lat_in.shape[0]
    spread_lane = lax.broadcasted_iota(jnp.int32, (lat_count, 128), 1)
    spread_row = lax.broadcasted_iota(jnp.int32, (lat_count, 128), 0)
    for f in range(frames):
        hit = (lax.rem(spread_lane, lat_count) == spread_row) & (
            lax.div(spread_lane, 64) == f
        )
        lat_ref[f] = lax.dot_general(
            lat_in[...],
            jnp.where(hit, 1.0, 0.0).astype(jnp.bfloat16),
            (((0,), (0,)), ((), ())),
            preferred_element_type=jnp.float32,
        ).astype(jnp.bfloat16)

    @pl.loop(0, rows)
    def _(r):
        for f in range(frames):
            values = x_ref[f, r].astype(jnp.float32)
            ext_one[2 + f, r + 1] = activate(values, gain_one).astype(jnp.bfloat16)

    peers = bands - 1
    for there, _, _ in links:
        peers = peers + jnp.where(there, 1, 0)
    pl.semaphore_wait(barrier, peers)

    def halo(sec, ext):
        sends = (
            (has_next, ext.at[frames : frames + 2, 1 : rows + 1], ext.at[0:2, 1 : rows + 1], 1, 0),
            (has_up, ext.at[2 : frames + 2, 1], ext.at[2 : frames + 2, rows + 1], 0, -1),
            (has_down, ext.at[2 : frames + 2, rows], ext.at[2 : frames + 2, 0], 0, 1),
            (has_next & has_up, ext.at[frames : frames + 2, 1], ext.at[0:2, rows + 1], 1, -1),
            (has_next & has_down, ext.at[frames : frames + 2, rows], ext.at[0:2, 0], 1, 1),
        )
        waits = (has_prev, has_down, has_up, has_prev & has_down, has_prev & has_up)
        made = []
        for k, (there, src, dst, dt, ds) in enumerate(sends):
            copy = pltpu.make_async_remote_copy(
                src_ref=src,
                dst_ref=dst,
                send_sem=halo_send.at[sec, k],
                recv_sem=halo_recv.at[sec, k],
                device_id={"tm": time + dt, "space": place + ds},
                device_id_type=MESH,
            )
            made.append((there, waits[k], copy))
        return made

    def start_all(made):
        for k in (1, 2, 3, 4, 0):
            there, _, copy = made[k]

            @pl.when(there)
            def _():
                copy.start()

    def finish_recv(made):
        for _, here, copy in made:

            @pl.when(here)
            def _():
                copy.wait_recv()

    def finish_send(made):
        for there, _, copy in made:

            @pl.when(there)
            def _():
                copy.wait_send()

    col_id = lax.broadcasted_iota(jnp.int32, (cols, chans), 0)
    size = ROW_BLOCK * cols

    def conv_rows(ext, weight, r0, f):
        lhs = jnp.concatenate(
            [
                ext[f + kt, pl.ds(r0 + ky, ROW_BLOCK)].reshape(size, chans)
                for kt in range(3)
                for ky in range(3)
            ],
            axis=1,
        )
        taps = [
            jnp.dot(
                lhs,
                weight[kx].reshape(9 * chans, chans),
                preferred_element_type=jnp.float32,
            )
            for kx in range(3)
        ]
        done = []
        for k in range(ROW_BLOCK):
            left, mid, right = (tap[k * cols : (k + 1) * cols] for tap in taps)
            left = jnp.where(col_id == 0, 0.0, pltpu.roll(left, 1, 0))
            right = jnp.where(col_id == cols - 1, 0.0, pltpu.roll(right, cols - 1, 0))
            done.append(mid + left + right)
        return done

    halo_one = halo(0, ext_one)
    start_all(halo_one)
    for copy in weight_copies[0]:
        copy.wait()
    finish_recv(halo_one)

    @pl.loop(0, rows // ROW_BLOCK)
    def _(block):
        r0 = block * ROW_BLOCK
        for f in range(frames):
            for k, update in enumerate(conv_rows(ext_one, w_one, r0, f)):
                total = x_ref[f, r0 + k].astype(jnp.float32) + update
                rounded = total.astype(jnp.bfloat16)
                mid_stream[f, r0 + k] = rounded
                ext_two[2 + f, r0 + k + 1] = activate(
                    rounded.astype(jnp.float32), gain_two
                ).astype(jnp.bfloat16)

    halo_two = halo(1, ext_two)
    start_all(halo_two)
    for copy in weight_copies[1]:
        copy.wait()
    finish_recv(halo_two)

    @pl.loop(0, rows // ROW_BLOCK)
    def _(block):
        r0 = block * ROW_BLOCK
        latents = [jnp.zeros((cols, 128), jnp.float32)] * ROW_BLOCK
        for f in range(frames):
            for k, update in enumerate(conv_rows(ext_two, w_two, r0, f)):
                total = mid_stream[f, r0 + k].astype(jnp.float32) + update
                final = activate(
                    total.astype(jnp.bfloat16).astype(jnp.float32), gain_out
                ).astype(jnp.bfloat16)
                latents[k] = latents[k] + jnp.dot(
                    final, lat_ref[f], preferred_element_type=jnp.float32
                )
        for k in range(ROW_BLOCK):
            lat_rows[r0 + k] = latents[k]

    finish_send(halo_one)
    finish_send(halo_two)

    clip = lax.div(first, clip_len)
    limit = clip_ref[clip]

    def pyramid(source, count, width, patch_rows, pooled):
        lane = lax.broadcasted_iota(jnp.int32, (width, 128), 1)
        group = lax.rem(lax.div(lane, 16), 4)
        position = first - clip * clip_len + lax.div(lane, 64)
        keep = position < limit
        for i in range(count):
            total = None
            chosen = None
            for p in range(2):
                for q in range(2):
                    part = source[2 * i + p, pl.ds(q, width, stride=2), :]
                    total = part if total is None else total + part
                    chosen = (
                        part
                        if chosen is None
                        else jnp.where(group == 2 * p + q, part, chosen)
                    )
            patch_rows[i] = jnp.where(keep, chosen, 0.0)
            if pooled is not None:
                pooled[i] = total * 0.25

    levels = (
        (lat_rows, fine_rows, pool_mid, fine_bands),
        (pool_mid, mid_rows, pool_coarse, mid_bands),
        (pool_coarse, coarse_rows, None, coarse_bands),
    )
    stage[...] = jnp.zeros_like(stage)
    offset = 0
    for level, (source, patch_rows, pooled, by_band) in enumerate(levels):
        count, width, _ = patch_rows.shape
        pyramid(source, count, width, patch_rows, pooled)
        each = width // bands
        for b in range(bands):
            for i in range(count):
                by_band[b, i * each : (i + 1) * each] = patch_rows[
                    i, b * each : (b + 1) * each
                ]
        for d in range(bands):
            stage[d, offset : offset + count * each] = by_band[maps_ref[level, d]]
        offset += count * each
    for d in range(bands):
        send_buf[d] = stage[d].astype(jnp.bfloat16)

    moves = []
    for step in range(1, bands):
        target = lax.rem(place + step, bands)
        copy = pltpu.make_async_remote_copy(
            src_ref=send_buf.at[target],
            dst_ref=recv_buf.at[place],
            send_sem=band_send.at[step - 1],
            recv_sem=band_recv.at[step - 1],
            device_id={"tm": time, "space": target},
            device_id_type=MESH,
        )
        copy.start()
        moves.append(copy)
    recv_buf[place] = send_buf[place]
    for copy in moves:
        copy.wait_recv()
    for copy in moves:
        copy.wait_send()
    for d in range(bands):
        got = recv_buf[d].astype(jnp.float32)
        offset = 0
        for out_ref in (fine_out, mid_out, coarse_out):
            each = out_ref.shape[0] // bands
            out_ref[d * each : (d + 1) * each] = got[offset : offset + each]
            offset += each


def encode(features, clip_frames, band_maps, gains, latents, conv_one, conv_two, clip_len):
    bands = lax.axis_size("space")
    frames, rows, cols, chans = features.shape
    counts = [(rows // s // 2, cols // s // 2) for s in (1, 2, 4)]
    used = sum(n * w // bands for n, w in counts)
    message = -(-used // 16) * 16
    f32, bf16 = jnp.float32, jnp.bfloat16
    vmem = pl.BlockSpec(memory_space=pltpu.VMEM)
    hbm = pl.BlockSpec(memory_space=pltpu.HBM)
    weight = pltpu.VMEM((3, 9, chans, chans), bf16)
    ext = pltpu.VMEM((frames + 2, rows + 2, cols, chans), bf16)
    stream = pltpu.VMEM((frames, rows, cols, chans), bf16)
    gain = pltpu.VMEM((1, chans), f32)
    scratch = [
        pltpu.SMEM(clip_frames.shape, jnp.int32),
        pltpu.SMEM(band_maps.shape, jnp.int32),
        stream,
        gain,
        gain,
        gain,
        pltpu.VMEM(latents.shape, bf16),
        pltpu.VMEM((frames, chans, 128), bf16),
    ]
    scratch += [weight, weight, ext, ext, stream]
    scratch.append(pltpu.VMEM((rows, cols, 128), f32))
    scratch += [pltpu.VMEM((n, w, 128), f32) for n, w in counts]
    scratch += [pltpu.VMEM((n, w, 128), f32) for n, w in counts[:2]]
    scratch += [pltpu.VMEM((bands, n * w // bands, 128), f32) for n, w in counts]
    scratch += [
        pltpu.VMEM((bands, message, 128), f32),
        pltpu.VMEM((bands, message, 128), bf16),
        pltpu.VMEM((bands, message, 128), bf16),
        pltpu.SemaphoreType.DMA((7,)),
        pltpu.SemaphoreType.DMA((2, 3)),
        pltpu.SemaphoreType.DMA((2, 5)),
        pltpu.SemaphoreType.DMA((2, 5)),
        pltpu.SemaphoreType.DMA((bands - 1,)),
        pltpu.SemaphoreType.DMA((bands - 1,)),
    ]
    return pl.pallas_call(
        functools.partial(encoder_kernel, clip_len, bands),
        out_shape=[jax.ShapeDtypeStruct((n * w, 128), f32) for n, w in counts],
        in_specs=[hbm] * 9,
        out_specs=[vmem] * 3,
        scratch_shapes=scratch,
        compiler_params=pltpu.CompilerParams(
            collective_id=0, has_side_effects=True, vmem_limit_bytes=63 * 1024 * 1024
        ),
        name="encoder",
    )(clip_frames, band_maps, features, *gains, latents, conv_one, conv_two)


def embed_kernel(fine_ref, mid_ref, coarse_ref, weight_ref, *out_refs):
    weight = weight_ref[...]
    blank = jnp.zeros_like(weight)
    for f in range(out_refs[0].shape[0]):
        halves = [blank, blank]
        halves[f] = weight
        padded = jnp.concatenate(halves, axis=0)
        for source, out_ref in zip((fine_ref, mid_ref, coarse_ref), out_refs):
            tokens = jnp.dot(
                source[...].astype(jnp.bfloat16), padded, preferred_element_type=jnp.float32
            )
            _, _, token_rows, each, wide = out_ref.shape
            if each % 8 == 0:
                out_ref[f, 0] = tokens.reshape(token_rows, each, wide).astype(jnp.bfloat16)
            else:
                for i in range(token_rows):
                    out_ref[f, 0, i] = tokens[i * each : (i + 1) * each].astype(jnp.bfloat16)


def embed(patches, embed_weight, frames, bands, shapes):
    depth, hidden = embed_weight.shape
    steps = 4
    wide = hidden // steps
    whole = lambda h: (0, 0)
    out_shape, out_specs = [], []
    for token_rows, each in shapes:
        out_shape.append(
            jax.ShapeDtypeStruct((frames, 1, token_rows, each, hidden), jnp.bfloat16)
        )
        out_specs.append(
            pl.BlockSpec((frames, 1, token_rows, each, wide), lambda h: (0, 0, 0, 0, h))
        )
    return pl.pallas_call(
        embed_kernel,
        grid=(steps,),
        out_shape=out_shape,
        in_specs=[pl.BlockSpec(p.shape, whole) for p in patches]
        + [pl.BlockSpec((depth, wide), lambda h: (0, h))],
        out_specs=out_specs,
        compiler_params=pltpu.CompilerParams(vmem_limit_bytes=32 * 1024 * 1024),
        name="embed",
    )(*patches, embed_weight)


def body(
    features,
    clip_frames,
    band_maps,
    gain_one,
    conv_one,
    gain_two,
    conv_two,
    gain_out,
    latent_weight,
    embed_weight,
):
    frames, rows, cols, chans = features.shape
    clip_len = frames * lax.axis_size("tm") // 2
    bands = lax.axis_size("space")
    patches = encode(
        features,
        clip_frames,
        band_maps,
        [g.reshape(1, chans) for g in (gain_one, gain_two, gain_out)],
        latent_weight.T,
        conv_one.reshape(9, 3, chans, chans),
        conv_two.reshape(9, 3, chans, chans),
        clip_len,
    )
    shapes = [(bands * (rows // s // 2), cols // s // 2 // bands) for s in (1, 2, 4)]
    return tuple(embed(patches, embed_weight, frames, bands, shapes))


def solution(mesh):
    return jax.shard_map(
        body,
        mesh=mesh,
        in_specs=(P("tm", "space", None, None), P(), P(), P(), P(), P(), P(), P(), P(), P()),
        out_specs=(
            P("tm", "space", None, None, None),
            P("tm", "space", None, None, None),
            P("tm", "space", None, None, None),
        ),
        check_vma=False,
    )
```

```python
import functools

import jax
import jax.numpy as jnp
from jax import lax
from jax.experimental import pallas as pl
from jax.experimental.pallas import tpu as pltpu
from jax.sharding import PartitionSpec as P

MESH = pl.DeviceIdType.MESH

def activate(values, gain_row):
    meansq = jnp.mean(values * values, axis=-1, keepdims=True)
    half = values * lax.rsqrt(meansq + 1e-06) * (gain_row * 0.5)
    return half + half * jnp.tanh(half)


def encoder_kernel(
    clip_len,
    bands,
    clip_hbm,
    maps_hbm,
    x_hbm,
    g1_hbm,
    g2_hbm,
    g3_hbm,
    lat_hbm,
    w1_hbm,
    w2_hbm,
    fine_out,
    mid_out,
    coarse_out,
    clip_ref,
    maps_ref,
    x_ref,
    g1_ref,
    g2_ref,
    g3_ref,
    lat_in,
    lat_ref,
    w_one,
    w_two,
    ext_one,
    ext_two,
    mid_stream,
    lat_rows,
    fine_rows,
    mid_rows,
    coarse_rows,
    pool_mid,
    pool_coarse,
    fine_bands,
    mid_bands,
    coarse_bands,
    stage,
    send_buf,
    recv_buf,
    in_sem,
    w_sem,
    halo_send,
    halo_recv,
    band_send,
    band_recv,
):
    frames, rows, cols, chans = x_ref.shape
    time = lax.axis_index("tm")
    place = lax.axis_index("space")
    first = time * frames
    has_prev = lax.rem(first, clip_len) != 0
    has_next = lax.rem(first + frames, clip_len) != 0
    has_up = place > 0
    has_down = place < bands - 1

    weight_copies = [
        [
            pltpu.make_async_copy(src.at[:, kx], dst.at[kx], w_sem.at[sec, kx])
            for kx in range(3)
        ]
        for sec, (src, dst) in enumerate(((w1_hbm, w_one), (w2_hbm, w_two)))
    ]
    pairs = (
        (x_hbm, x_ref),
        (g1_hbm, g1_ref),
        (g2_hbm, g2_ref),
        (g3_hbm, g3_ref),
        (lat_hbm, lat_in),
        (clip_hbm, clip_ref),
        (maps_hbm, maps_ref),
    )
    small_copies = [
        pltpu.make_async_copy(src, dst, in_sem.at[k]) for k, (src, dst) in enumerate(pairs)
    ]
    for copy in small_copies:
        copy.start()
    for group in weight_copies:
        for copy in group:
            copy.start()

    barrier = pltpu.get_barrier_semaphore()
    links = [
        (has_next, time + 1, place),
        (has_prev, time - 1, place),
        (has_next & has_up, time + 1, place - 1),
        (has_next & has_down, time + 1, place + 1),
        (has_prev & has_up, time - 1, place - 1),
        (has_prev & has_down, time - 1, place + 1),
    ]
    for there, t, s in links:

        @pl.when(there)
        def _():
            pl.semaphore_signal(
                barrier, inc=1, device_id={"tm": t, "space": s}, device_id_type=MESH
            )

    for step in range(1, bands):
        pl.semaphore_signal(
            barrier,
            inc=1,
            device_id={"tm": time, "space": lax.rem(place + step, bands)},
            device_id_type=MESH,
        )

    for ext in (ext_one, ext_two):

        @pl.when(jnp.logical_not(has_prev))
        def _():
            ext[0:2] = jnp.zeros((2, rows + 2, cols, chans), jnp.bfloat16)

        @pl.when(jnp.logical_not(has_up))
        def _():
            ext[:, 0] = jnp.zeros((frames + 2, cols, chans), jnp.bfloat16)

        @pl.when(jnp.logical_not(has_down))
        def _():
            ext[:, rows + 1] = jnp.zeros((frames + 2, cols, chans), jnp.bfloat16)

    for copy in small_copies:
        copy.wait()
    gain_one = g1_ref[...]
    gain_two = g2_ref[...]
    gain_out = g3_ref[...]

    lat_count = lat_in.shape[0]
    spread_lane = lax.broadcasted_iota(jnp.int32, (lat_count, 128), 1)
    spread_row = lax.broadcasted_iota(jnp.int32, (lat_count, 128), 0)
    for f in range(frames):
        hit = (lax.rem(spread_lane, lat_count) == spread_row) & (
            lax.div(spread_lane, 64) == f
        )
        lat_ref[f] = lax.dot_general(
            lat_in[...],
            jnp.where(hit, 1.0, 0.0).astype(jnp.bfloat16),
            (((0,), (0,)), ((), ())),
            preferred_element_type=jnp.float32,
        ).astype(jnp.bfloat16)

    def activate_row(r):
        for f in range(frames):
            values = x_ref[f, r].astype(jnp.float32)
            ext_one[2 + f, r + 1] = activate(values, gain_one).astype(jnp.bfloat16)

    activate_row(0)
    activate_row(rows - 1)

    peers = bands - 1
    for there, _, _ in links:
        peers = peers + jnp.where(there, 1, 0)
    pl.semaphore_wait(barrier, peers)

    def halo(sec, ext):
        last, own = slice(frames, frames + 2), slice(2, frames + 2)
        old = slice(0, 2)
        low, high = rows, rows + 1
        sends = (
            (has_next, ext.at[last, 2:rows], ext.at[old, 2:rows], 1, 0),
            (has_up, ext.at[own, 1], ext.at[own, high], 0, -1),
            (has_down, ext.at[own, low], ext.at[own, 0], 0, 1),
            (has_next & has_up, ext.at[last, 1], ext.at[old, high], 1, -1),
            (has_next & has_down, ext.at[last, low], ext.at[old, 0], 1, 1),
            (has_next, ext.at[last, 1], ext.at[old, 1], 1, 0),
            (has_next, ext.at[last, low], ext.at[old, low], 1, 0),
        )
        waits = (
            has_prev,
            has_down,
            has_up,
            has_prev & has_down,
            has_prev & has_up,
            has_prev,
            has_prev,
        )
        made = []
        for k, (there, src, dst, dt, ds) in enumerate(sends):
            copy = pltpu.make_async_remote_copy(
                src_ref=src,
                dst_ref=dst,
                send_sem=halo_send.at[sec, k],
                recv_sem=halo_recv.at[sec, k],
                device_id={"tm": time + dt, "space": place + ds},
                device_id_type=MESH,
            )
            made.append((there, waits[k], copy))
        return made

    def start(made, which):
        for k in which:
            there, _, copy = made[k]

            @pl.when(there)
            def _():
                copy.start()

    def finish_recv(made, which):
        for k in which:
            _, here, copy = made[k]

            @pl.when(here)
            def _():
                copy.wait_recv()

    def finish_send(made):
        for there, _, copy in made:

            @pl.when(there)
            def _():
                copy.wait_send()

    col_id = lax.broadcasted_iota(jnp.int32, (cols, chans), 0)
    interior = rows - 2
    row_block = max(n for n in (1, 2, 3) if interior % n == 0)
    ends = (0, rows - 1)
    inner, edges, across = (0,), (1, 2, 3, 4, 5, 6), (1, 2, 3, 4)

    def conv_rows(ext, weight, which, f):
        lhs = jnp.concatenate(
            [
                jnp.concatenate([ext[f + kt, r + ky] for r in which], axis=0)
                for kt in range(3)
                for ky in range(3)
            ],
            axis=1,
        )
        taps = [
            jnp.dot(
                lhs,
                weight[kx].reshape(9 * chans, chans),
                preferred_element_type=jnp.float32,
            )
            for kx in range(3)
        ]
        done = []
        for k in range(len(which)):
            left, mid, right = (tap[k * cols : (k + 1) * cols] for tap in taps)
            left = jnp.where(col_id == 0, 0.0, pltpu.roll(left, 1, 0))
            right = jnp.where(col_id == cols - 1, 0.0, pltpu.roll(right, cols - 1, 0))
            done.append(mid + left + right)
        return done

    def first_section(which):
        for f in range(frames):
            for r, update in zip(which, conv_rows(ext_one, w_one, which, f)):
                total = x_ref[f, r].astype(jnp.float32) + update
                rounded = total.astype(jnp.bfloat16)
                mid_stream[f, r] = rounded
                ext_two[2 + f, r + 1] = activate(
                    rounded.astype(jnp.float32), gain_two
                ).astype(jnp.bfloat16)

    def second_section(which):
        latents = [jnp.zeros((cols, 128), jnp.float32) for _ in which]
        for f in range(frames):
            for k, update in enumerate(conv_rows(ext_two, w_two, which, f)):
                total = mid_stream[f, which[k]].astype(jnp.float32) + update
                final = activate(
                    total.astype(jnp.bfloat16).astype(jnp.float32), gain_out
                ).astype(jnp.bfloat16)
                latents[k] = latents[k] + jnp.dot(
                    final, lat_ref[f], preferred_element_type=jnp.float32
                )
        for r, latent in zip(which, latents):
            lat_rows[r] = latent

    def interior_rows(section):
        @pl.loop(0, interior // row_block)
        def _(block):
            section([1 + block * row_block + k for k in range(row_block)])

    halo_one = halo(0, ext_one)
    halo_two = halo(1, ext_two)
    start(halo_one, edges)

    @pl.loop(1, rows - 1)
    def _(r):
        activate_row(r)

    start(halo_one, inner)
    for copy in weight_copies[0]:
        copy.wait()
    finish_recv(halo_one, (0, 5, 6))
    interior_rows(first_section)
    start(halo_two, inner)
    finish_recv(halo_one, across)
    first_section(ends)
    start(halo_two, edges)
    for copy in weight_copies[1]:
        copy.wait()
    finish_recv(halo_two, (0, 5, 6))
    interior_rows(second_section)
    finish_recv(halo_two, across)
    second_section(ends)

    finish_send(halo_one)
    finish_send(halo_two)

    clip = lax.div(first, clip_len)
    limit = clip_ref[clip]

    def pyramid(source, count, width, patch_rows, pooled):
        lane = lax.broadcasted_iota(jnp.int32, (width, 128), 1)
        group = lax.rem(lax.div(lane, 16), 4)
        position = first - clip * clip_len + lax.div(lane, 64)
        keep = position < limit
        for i in range(count):
            total = None
            chosen = None
            for p in range(2):
                for q in range(2):
                    part = source[2 * i + p, pl.ds(q, width, stride=2), :]
                    total = part if total is None else total + part
                    chosen = (
                        part
                        if chosen is None
                        else jnp.where(group == 2 * p + q, part, chosen)
                    )
            patch_rows[i] = jnp.where(keep, chosen, 0.0)
            if pooled is not None:
                pooled[i] = total * 0.25

    levels = (
        (lat_rows, fine_rows, pool_mid, fine_bands),
        (pool_mid, mid_rows, pool_coarse, mid_bands),
        (pool_coarse, coarse_rows, None, coarse_bands),
    )
    stage[...] = jnp.zeros_like(stage)
    offset = 0
    for level, (source, patch_rows, pooled, by_band) in enumerate(levels):
        count, width, _ = patch_rows.shape
        pyramid(source, count, width, patch_rows, pooled)
        each = width // bands
        for b in range(bands):
            for i in range(count):
                by_band[b, i * each : (i + 1) * each] = patch_rows[
                    i, b * each : (b + 1) * each
                ]
        for d in range(bands):
            stage[d, offset : offset + count * each] = by_band[maps_ref[level, d]]
        offset += count * each
    for d in range(bands):
        send_buf[d] = stage[d].astype(jnp.bfloat16)

    moves = []
    for step in range(1, bands):
        target = lax.rem(place + step, bands)
        copy = pltpu.make_async_remote_copy(
            src_ref=send_buf.at[target],
            dst_ref=recv_buf.at[place],
            send_sem=band_send.at[step - 1],
            recv_sem=band_recv.at[step - 1],
            device_id={"tm": time, "space": target},
            device_id_type=MESH,
        )
        copy.start()
        moves.append(copy)
    recv_buf[place] = send_buf[place]
    for copy in moves:
        copy.wait_recv()
    for copy in moves:
        copy.wait_send()
    for d in range(bands):
        got = recv_buf[d].astype(jnp.float32)
        offset = 0
        for out_ref in (fine_out, mid_out, coarse_out):
            each = out_ref.shape[0] // bands
            out_ref[d * each : (d + 1) * each] = got[offset : offset + each]
            offset += each


def encode(features, clip_frames, band_maps, gains, latents, conv_one, conv_two, clip_len):
    bands = lax.axis_size("space")
    frames, rows, cols, chans = features.shape
    counts = [(rows // s // 2, cols // s // 2) for s in (1, 2, 4)]
    used = sum(n * w // bands for n, w in counts)
    message = -(-used // 16) * 16
    f32, bf16 = jnp.float32, jnp.bfloat16
    vmem = pl.BlockSpec(memory_space=pltpu.VMEM)
    hbm = pl.BlockSpec(memory_space=pltpu.HBM)
    weight = pltpu.VMEM((3, 9, chans, chans), bf16)
    ext = pltpu.VMEM((frames + 2, rows + 2, cols, chans), bf16)
    stream = pltpu.VMEM((frames, rows, cols, chans), bf16)
    gain = pltpu.VMEM((1, chans), f32)
    scratch = [
        pltpu.SMEM(clip_frames.shape, jnp.int32),
        pltpu.SMEM(band_maps.shape, jnp.int32),
        stream,
        gain,
        gain,
        gain,
        pltpu.VMEM(latents.shape, bf16),
        pltpu.VMEM((frames, chans, 128), bf16),
    ]
    scratch += [weight, weight, ext, ext, stream]
    scratch.append(pltpu.VMEM((rows, cols, 128), f32))
    scratch += [pltpu.VMEM((n, w, 128), f32) for n, w in counts]
    scratch += [pltpu.VMEM((n, w, 128), f32) for n, w in counts[:2]]
    scratch += [pltpu.VMEM((bands, n * w // bands, 128), f32) for n, w in counts]
    scratch += [
        pltpu.VMEM((bands, message, 128), f32),
        pltpu.VMEM((bands, message, 128), bf16),
        pltpu.VMEM((bands, message, 128), bf16),
        pltpu.SemaphoreType.DMA((7,)),
        pltpu.SemaphoreType.DMA((2, 3)),
        pltpu.SemaphoreType.DMA((2, 7)),
        pltpu.SemaphoreType.DMA((2, 7)),
        pltpu.SemaphoreType.DMA((bands - 1,)),
        pltpu.SemaphoreType.DMA((bands - 1,)),
    ]
    return pl.pallas_call(
        functools.partial(encoder_kernel, clip_len, bands),
        out_shape=[jax.ShapeDtypeStruct((n * w, 128), f32) for n, w in counts],
        in_specs=[hbm] * 9,
        out_specs=[vmem] * 3,
        scratch_shapes=scratch,
        compiler_params=pltpu.CompilerParams(
            collective_id=0, has_side_effects=True, vmem_limit_bytes=63 * 1024 * 1024
        ),
        name="encoder",
    )(clip_frames, band_maps, features, *gains, latents, conv_one, conv_two)


def embed_kernel(fine_ref, mid_ref, coarse_ref, weight_ref, *out_refs):
    weight = weight_ref[...]
    blank = jnp.zeros_like(weight)
    for f in range(out_refs[0].shape[0]):
        halves = [blank, blank]
        halves[f] = weight
        padded = jnp.concatenate(halves, axis=0)
        for source, out_ref in zip((fine_ref, mid_ref, coarse_ref), out_refs):
            tokens = jnp.dot(
                source[...].astype(jnp.bfloat16), padded, preferred_element_type=jnp.float32
            )
            _, _, token_rows, each, wide = out_ref.shape
            if each % 8 == 0:
                out_ref[f, 0] = tokens.reshape(token_rows, each, wide).astype(jnp.bfloat16)
            else:
                for i in range(token_rows):
                    out_ref[f, 0, i] = tokens[i * each : (i + 1) * each].astype(jnp.bfloat16)


def embed(patches, embed_weight, frames, bands, shapes):
    depth, hidden = embed_weight.shape
    steps = 4
    wide = hidden // steps
    whole = lambda h: (0, 0)
    out_shape, out_specs = [], []
    for token_rows, each in shapes:
        out_shape.append(
            jax.ShapeDtypeStruct((frames, 1, token_rows, each, hidden), jnp.bfloat16)
        )
        out_specs.append(
            pl.BlockSpec((frames, 1, token_rows, each, wide), lambda h: (0, 0, 0, 0, h))
        )
    return pl.pallas_call(
        embed_kernel,
        grid=(steps,),
        out_shape=out_shape,
        in_specs=[pl.BlockSpec(p.shape, whole) for p in patches]
        + [pl.BlockSpec((depth, wide), lambda h: (0, h))],
        out_specs=out_specs,
        compiler_params=pltpu.CompilerParams(vmem_limit_bytes=63 * 1024 * 1024),
        name="embed",
    )(*patches, embed_weight)


def body(
    features,
    clip_frames,
    band_maps,
    gain_one,
    conv_one,
    gain_two,
    conv_two,
    gain_out,
    latent_weight,
    embed_weight,
):
    frames, rows, cols, chans = features.shape
    clip_len = frames * lax.axis_size("tm") // 2
    bands = lax.axis_size("space")
    patches = encode(
        features,
        clip_frames,
        band_maps,
        [g.reshape(1, chans) for g in (gain_one, gain_two, gain_out)],
        latent_weight.T,
        conv_one.reshape(9, 3, chans, chans),
        conv_two.reshape(9, 3, chans, chans),
        clip_len,
    )
    shapes = [(bands * (rows // s // 2), cols // s // 2 // bands) for s in (1, 2, 4)]
    return tuple(embed(patches, embed_weight, frames, bands, shapes))


def solution(mesh):
    return jax.shard_map(
        body,
        mesh=mesh,
        in_specs=(P("tm", "space", None, None), P(), P(), P(), P(), P(), P(), P(), P(), P()),
        out_specs=(
            P("tm", "space", None, None, None),
            P("tm", "space", None, None, None),
            P("tm", "space", None, None, None),
        ),
        check_vma=False,
    )
```

```python
import functools

import jax
import jax.numpy as jnp
from jax import lax
from jax.experimental import pallas as pl
from jax.experimental.pallas import tpu as pltpu
from jax.sharding import PartitionSpec as P

MESH = pl.DeviceIdType.MESH

def activate(values, gain_row):
    meansq = jnp.mean(values * values, axis=-1, keepdims=True)
    half = values * lax.rsqrt(meansq + 1e-06) * (gain_row * 0.5)
    return half + half * jnp.tanh(half)


def encoder_kernel(
    clip_len,
    bands,
    clip_hbm,
    maps_hbm,
    x_hbm,
    g1_hbm,
    g2_hbm,
    g3_hbm,
    lat_hbm,
    w1_hbm,
    w2_hbm,
    fine_out,
    mid_out,
    coarse_out,
    clip_ref,
    maps_ref,
    x_ref,
    g1_ref,
    g2_ref,
    g3_ref,
    lat_in,
    lat_ref,
    w_one,
    w_two,
    ext_one,
    ext_two,
    mid_stream,
    lat_rows,
    fine_rows,
    mid_rows,
    coarse_rows,
    pool_mid,
    pool_coarse,
    fine_bands,
    mid_bands,
    coarse_bands,
    stage,
    send_buf,
    recv_buf,
    in_sem,
    w_sem,
    halo_send,
    halo_recv,
    band_send,
    band_recv,
):
    frames, rows, cols, chans = x_ref.shape
    time = lax.axis_index("tm")
    place = lax.axis_index("space")
    first = time * frames
    has_prev = lax.rem(first, clip_len) != 0
    has_next = lax.rem(first + frames, clip_len) != 0
    has_up = place > 0
    has_down = place < bands - 1

    weight_copies = [
        [
            pltpu.make_async_copy(src.at[:, kx], dst.at[kx], w_sem.at[sec, kx])
            for kx in range(3)
        ]
        for sec, (src, dst) in enumerate(((w1_hbm, w_one), (w2_hbm, w_two)))
    ]
    pairs = (
        (x_hbm, x_ref),
        (g1_hbm, g1_ref),
        (g2_hbm, g2_ref),
        (g3_hbm, g3_ref),
        (lat_hbm, lat_in),
        (clip_hbm, clip_ref),
        (maps_hbm, maps_ref),
    )
    small_copies = [
        pltpu.make_async_copy(src, dst, in_sem.at[k]) for k, (src, dst) in enumerate(pairs)
    ]
    for copy in small_copies:
        copy.start()
    for group in weight_copies:
        for copy in group:
            copy.start()

    barrier = pltpu.get_barrier_semaphore()
    links = [
        (has_next, time + 1, place),
        (has_prev, time - 1, place),
        (has_next & has_up, time + 1, place - 1),
        (has_next & has_down, time + 1, place + 1),
        (has_prev & has_up, time - 1, place - 1),
        (has_prev & has_down, time - 1, place + 1),
    ]
    for there, t, s in links:

        @pl.when(there)
        def _():
            pl.semaphore_signal(
                barrier, inc=1, device_id={"tm": t, "space": s}, device_id_type=MESH
            )

    for step in range(1, bands):
        pl.semaphore_signal(
            barrier,
            inc=1,
            device_id={"tm": time, "space": lax.rem(place + step, bands)},
            device_id_type=MESH,
        )

    for ext in (ext_one, ext_two):

        @pl.when(jnp.logical_not(has_prev))
        def _():
            ext[0:2] = jnp.zeros((2, rows + 2, cols, chans), jnp.bfloat16)

        @pl.when(jnp.logical_not(has_up))
        def _():
            ext[:, 0] = jnp.zeros((frames + 2, cols, chans), jnp.bfloat16)

        @pl.when(jnp.logical_not(has_down))
        def _():
            ext[:, rows + 1] = jnp.zeros((frames + 2, cols, chans), jnp.bfloat16)

    for copy in small_copies:
        copy.wait()
    gain_one = g1_ref[...]
    gain_two = g2_ref[...]
    gain_out = g3_ref[...]

    lat_count = lat_in.shape[0]
    spread_lane = lax.broadcasted_iota(jnp.int32, (lat_count, 128), 1)
    spread_row = lax.broadcasted_iota(jnp.int32, (lat_count, 128), 0)
    for f in range(frames):
        hit = (lax.rem(spread_lane, lat_count) == spread_row) & (
            lax.div(spread_lane, 64) == f
        )
        lat_ref[f] = lax.dot_general(
            lat_in[...],
            jnp.where(hit, 1.0, 0.0).astype(jnp.bfloat16),
            (((0,), (0,)), ((), ())),
            preferred_element_type=jnp.float32,
        ).astype(jnp.bfloat16)

    def activate_row(r):
        for f in range(frames):
            values = x_ref[f, r].astype(jnp.float32)
            ext_one[2 + f, r + 1] = activate(values, gain_one).astype(jnp.bfloat16)

    activate_row(0)
    activate_row(rows - 1)

    peers = bands - 1
    for there, _, _ in links:
        peers = peers + jnp.where(there, 1, 0)
    pl.semaphore_wait(barrier, peers)

    def halo(sec, ext):
        last, own = slice(frames, frames + 2), slice(2, frames + 2)
        old = slice(0, 2)
        low, high = rows, rows + 1
        sends = (
            (has_next, ext.at[last, 2:rows], ext.at[old, 2:rows], 1, 0),
            (has_up, ext.at[own, 1], ext.at[own, high], 0, -1),
            (has_down, ext.at[own, low], ext.at[own, 0], 0, 1),
            (has_next & has_up, ext.at[last, 1], ext.at[old, high], 1, -1),
            (has_next & has_down, ext.at[last, low], ext.at[old, 0], 1, 1),
            (has_next, ext.at[last, 1], ext.at[old, 1], 1, 0),
            (has_next, ext.at[last, low], ext.at[old, low], 1, 0),
        )
        waits = (
            has_prev,
            has_down,
            has_up,
            has_prev & has_down,
            has_prev & has_up,
            has_prev,
            has_prev,
        )
        made = []
        for k, (there, src, dst, dt, ds) in enumerate(sends):
            copy = pltpu.make_async_remote_copy(
                src_ref=src,
                dst_ref=dst,
                send_sem=halo_send.at[sec, k],
                recv_sem=halo_recv.at[sec, k],
                device_id={"tm": time + dt, "space": place + ds},
                device_id_type=MESH,
            )
            made.append((there, waits[k], copy))
        return made

    def start(made, which):
        for k in which:
            there, _, copy = made[k]

            @pl.when(there)
            def _():
                copy.start()

    def finish_recv(made, which):
        for k in which:
            _, here, copy = made[k]

            @pl.when(here)
            def _():
                copy.wait_recv()

    def finish_send(made):
        for there, _, copy in made:

            @pl.when(there)
            def _():
                copy.wait_send()

    col_id = lax.broadcasted_iota(jnp.int32, (cols, chans), 0)
    interior = rows - 2
    row_block = max(n for n in (1, 2, 3, 6) if interior % n == 0)
    ends = (0, rows - 1)
    inner, edges, across = (0,), (1, 2, 3, 4, 5, 6), (1, 2, 3, 4)

    def conv_rows(ext, weight, which, f):
        lhs = jnp.concatenate(
            [
                jnp.concatenate([ext[f + kt, r + ky] for r in which], axis=0)
                for kt in range(3)
                for ky in range(3)
            ],
            axis=1,
        )
        taps = [
            jnp.dot(
                lhs,
                weight[kx].reshape(9 * chans, chans),
                preferred_element_type=jnp.float32,
            )
            for kx in range(3)
        ]
        done = []
        for k in range(len(which)):
            left, mid, right = (tap[k * cols : (k + 1) * cols] for tap in taps)
            left = jnp.where(col_id == 0, 0.0, pltpu.roll(left, 1, 0))
            right = jnp.where(col_id == cols - 1, 0.0, pltpu.roll(right, cols - 1, 0))
            done.append(mid + left + right)
        return done

    def first_section(which):
        for f in range(frames):
            for r, update in zip(which, conv_rows(ext_one, w_one, which, f)):
                total = x_ref[f, r].astype(jnp.float32) + update
                rounded = total.astype(jnp.bfloat16)
                mid_stream[f, r] = rounded
                ext_two[2 + f, r + 1] = activate(
                    rounded.astype(jnp.float32), gain_two
                ).astype(jnp.bfloat16)

    def second_section(which):
        latents = [jnp.zeros((cols, 128), jnp.float32) for _ in which]
        for f in range(frames):
            for k, update in enumerate(conv_rows(ext_two, w_two, which, f)):
                total = mid_stream[f, which[k]].astype(jnp.float32) + update
                final = activate(
                    total.astype(jnp.bfloat16).astype(jnp.float32), gain_out
                ).astype(jnp.bfloat16)
                latents[k] = latents[k] + jnp.dot(
                    final, lat_ref[f], preferred_element_type=jnp.float32
                )
        for r, latent in zip(which, latents):
            lat_rows[r] = latent

    def interior_rows(section):
        @pl.loop(0, interior // row_block)
        def _(block):
            section([1 + block * row_block + k for k in range(row_block)])

    halo_one = halo(0, ext_one)
    halo_two = halo(1, ext_two)
    start(halo_one, edges)

    @pl.loop(1, rows - 1)
    def _(r):
        activate_row(r)

    start(halo_one, inner)
    for copy in weight_copies[0]:
        copy.wait()
    finish_recv(halo_one, (0, 5, 6))
    interior_rows(first_section)
    start(halo_two, inner)
    finish_recv(halo_one, across)
    first_section(ends)
    start(halo_two, edges)
    for copy in weight_copies[1]:
        copy.wait()
    finish_recv(halo_two, (0, 5, 6))
    interior_rows(second_section)
    finish_recv(halo_two, across)
    second_section(ends)

    finish_send(halo_one)
    finish_send(halo_two)

    clip = lax.div(first, clip_len)
    limit = clip_ref[clip]

    def pyramid(source, count, width, patch_rows, pooled):
        lane = lax.broadcasted_iota(jnp.int32, (width, 128), 1)
        group = lax.rem(lax.div(lane, 16), 4)
        position = first - clip * clip_len + lax.div(lane, 64)
        keep = position < limit
        for i in range(count):
            total = None
            chosen = None
            for p in range(2):
                for q in range(2):
                    part = source[2 * i + p, pl.ds(q, width, stride=2), :]
                    total = part if total is None else total + part
                    chosen = (
                        part
                        if chosen is None
                        else jnp.where(group == 2 * p + q, part, chosen)
                    )
            patch_rows[i] = jnp.where(keep, chosen, 0.0)
            if pooled is not None:
                pooled[i] = total * 0.25

    levels = (
        (lat_rows, fine_rows, pool_mid, fine_bands),
        (pool_mid, mid_rows, pool_coarse, mid_bands),
        (pool_coarse, coarse_rows, None, coarse_bands),
    )
    stage[...] = jnp.zeros_like(stage)
    offset = 0
    for level, (source, patch_rows, pooled, by_band) in enumerate(levels):
        count, width, _ = patch_rows.shape
        pyramid(source, count, width, patch_rows, pooled)
        each = width // bands
        for b in range(bands):
            for i in range(count):
                by_band[b, i * each : (i + 1) * each] = patch_rows[
                    i, b * each : (b + 1) * each
                ]
        for d in range(bands):
            stage[d, offset : offset + count * each] = by_band[maps_ref[level, d]]
        offset += count * each
    for d in range(bands):
        send_buf[d] = stage[d].astype(jnp.bfloat16)

    moves = []
    for step in range(1, bands):
        target = lax.rem(place + step, bands)
        copy = pltpu.make_async_remote_copy(
            src_ref=send_buf.at[target],
            dst_ref=recv_buf.at[place],
            send_sem=band_send.at[step - 1],
            recv_sem=band_recv.at[step - 1],
            device_id={"tm": time, "space": target},
            device_id_type=MESH,
        )
        copy.start()
        moves.append(copy)
    recv_buf[place] = send_buf[place]
    for copy in moves:
        copy.wait_recv()
    for copy in moves:
        copy.wait_send()
    for d in range(bands):
        got = recv_buf[d].astype(jnp.float32)
        offset = 0
        for out_ref in (fine_out, mid_out, coarse_out):
            each = out_ref.shape[0] // bands
            out_ref[d * each : (d + 1) * each] = got[offset : offset + each]
            offset += each


def encode(features, clip_frames, band_maps, gains, latents, conv_one, conv_two, clip_len):
    bands = lax.axis_size("space")
    frames, rows, cols, chans = features.shape
    counts = [(rows // s // 2, cols // s // 2) for s in (1, 2, 4)]
    used = sum(n * w // bands for n, w in counts)
    message = -(-used // 16) * 16
    f32, bf16 = jnp.float32, jnp.bfloat16
    vmem = pl.BlockSpec(memory_space=pltpu.VMEM)
    hbm = pl.BlockSpec(memory_space=pltpu.HBM)
    weight = pltpu.VMEM((3, 9, chans, chans), bf16)
    ext = pltpu.VMEM((frames + 2, rows + 2, cols, chans), bf16)
    stream = pltpu.VMEM((frames, rows, cols, chans), bf16)
    gain = pltpu.VMEM((1, chans), f32)
    scratch = [
        pltpu.SMEM(clip_frames.shape, jnp.int32),
        pltpu.SMEM(band_maps.shape, jnp.int32),
        stream,
        gain,
        gain,
        gain,
        pltpu.VMEM(latents.shape, bf16),
        pltpu.VMEM((frames, chans, 128), bf16),
    ]
    scratch += [weight, weight, ext, ext, stream]
    scratch.append(pltpu.VMEM((rows, cols, 128), f32))
    scratch += [pltpu.VMEM((n, w, 128), f32) for n, w in counts]
    scratch += [pltpu.VMEM((n, w, 128), f32) for n, w in counts[:2]]
    scratch += [pltpu.VMEM((bands, n * w // bands, 128), f32) for n, w in counts]
    scratch += [
        pltpu.VMEM((bands, message, 128), f32),
        pltpu.VMEM((bands, message, 128), bf16),
        pltpu.VMEM((bands, message, 128), bf16),
        pltpu.SemaphoreType.DMA((7,)),
        pltpu.SemaphoreType.DMA((2, 3)),
        pltpu.SemaphoreType.DMA((2, 7)),
        pltpu.SemaphoreType.DMA((2, 7)),
        pltpu.SemaphoreType.DMA((bands - 1,)),
        pltpu.SemaphoreType.DMA((bands - 1,)),
    ]
    return pl.pallas_call(
        functools.partial(encoder_kernel, clip_len, bands),
        out_shape=[jax.ShapeDtypeStruct((n * w, 128), f32) for n, w in counts],
        in_specs=[hbm] * 9,
        out_specs=[vmem] * 3,
        scratch_shapes=scratch,
        compiler_params=pltpu.CompilerParams(
            collective_id=0, has_side_effects=True, vmem_limit_bytes=63 * 1024 * 1024
        ),
        name="encoder",
    )(clip_frames, band_maps, features, *gains, latents, conv_one, conv_two)


def embed_kernel(fine_ref, mid_ref, coarse_ref, weight_ref, *out_refs):
    weight = weight_ref[...]
    blank = jnp.zeros_like(weight)
    for f in range(out_refs[0].shape[0]):
        halves = [blank, blank]
        halves[f] = weight
        padded = jnp.concatenate(halves, axis=0)
        for source, out_ref in zip((fine_ref, mid_ref, coarse_ref), out_refs):
            tokens = jnp.dot(
                source[...].astype(jnp.bfloat16), padded, preferred_element_type=jnp.float32
            )
            _, _, token_rows, each, wide = out_ref.shape
            if each % 8 == 0:
                out_ref[f, 0] = tokens.reshape(token_rows, each, wide).astype(jnp.bfloat16)
            else:
                for i in range(token_rows):
                    out_ref[f, 0, i] = tokens[i * each : (i + 1) * each].astype(jnp.bfloat16)


def embed(patches, embed_weight, frames, bands, shapes):
    depth, hidden = embed_weight.shape
    steps = 4
    wide = hidden // steps
    whole = lambda h: (0, 0)
    out_shape, out_specs = [], []
    for token_rows, each in shapes:
        out_shape.append(
            jax.ShapeDtypeStruct((frames, 1, token_rows, each, hidden), jnp.bfloat16)
        )
        out_specs.append(
            pl.BlockSpec((frames, 1, token_rows, each, wide), lambda h: (0, 0, 0, 0, h))
        )
    return pl.pallas_call(
        embed_kernel,
        grid=(steps,),
        out_shape=out_shape,
        in_specs=[pl.BlockSpec(p.shape, whole) for p in patches]
        + [pl.BlockSpec((depth, wide), lambda h: (0, h))],
        out_specs=out_specs,
        compiler_params=pltpu.CompilerParams(vmem_limit_bytes=63 * 1024 * 1024),
        name="embed",
    )(*patches, embed_weight)


def body(
    features,
    clip_frames,
    band_maps,
    gain_one,
    conv_one,
    gain_two,
    conv_two,
    gain_out,
    latent_weight,
    embed_weight,
):
    frames, rows, cols, chans = features.shape
    clip_len = frames * lax.axis_size("tm") // 2
    bands = lax.axis_size("space")
    patches = encode(
        features,
        clip_frames,
        band_maps,
        [g.reshape(1, chans) for g in (gain_one, gain_two, gain_out)],
        latent_weight.T,
        conv_one.reshape(9, 3, chans, chans),
        conv_two.reshape(9, 3, chans, chans),
        clip_len,
    )
    shapes = [(bands * (rows // s // 2), cols // s // 2 // bands) for s in (1, 2, 4)]
    return tuple(embed(patches, embed_weight, frames, bands, shapes))


def solution(mesh):
    return jax.shard_map(
        body,
        mesh=mesh,
        in_specs=(P("tm", "space", None, None), P(), P(), P(), P(), P(), P(), P(), P(), P()),
        out_specs=(
            P("tm", "space", None, None, None),
            P("tm", "space", None, None, None),
            P("tm", "space", None, None, None),
        ),
        check_vma=False,
    )
```
